256 devices in a mesh: ctx: 32 (over z_lo, x, y), tp: 4 (over z_hi), grp: 2 (over core).
Axes of the slice: x: 4, y: 4, z: 8 (z_hi: 4, z_lo: 2; z = z_hi * 2 + z_lo), core: 2. Of those that a mesh axis runs over, the one named last changes fastest.
Arguments:
- new_queries: bfloat16 [2048, 8, 1024], P('ctx', ('tp', 'grp')), may hold values from -8 to 8
- new_keys: bfloat16 [2048, 8, 128], P('ctx', ('tp', 'grp')), may hold values from -6 to 6
- new_values: bfloat16 [2048, 8, 128], P('ctx', ('tp', 'grp')), may hold values from -6 to 6
- cached_keys: bfloat16 [32768, 8, 128], P('ctx', ('tp', 'grp')), may hold values from -6 to 6
- cached_values: bfloat16 [32768, 8, 128], P('ctx', ('tp', 'grp')), may hold values from -6 to 6
- decode_queries: bfloat16 [128, 8, 1024], P('ctx', 'grp'), may hold values from -8 to 8
- decode_keys: bfloat16 [128, 2048, 8, 128], P('ctx', 'tp', 'grp'), may hold values from -6 to 6
- decode_values: bfloat16 [128, 2048, 8, 128], P('ctx', 'tp', 'grp'), may hold values from -6 to 6
- decode_lengths: int32 [128], P('ctx'), may hold values from 256 to 2048, as said below
- source_block: int32 [128], P('ctx'), may hold values from 0 to 31
Outputs:
- prefill_out: bfloat16 [2048, 8, 1024], P('ctx', ('tp', 'grp'))
- decode_out: bfloat16 [128, 8, 1024], P('ctx', 'grp')
The draws below stay inside these ranges and needn't reach their ends.
Inputs may be any that keep to these rules, and one draw needn't show every extreme that they name: `decode_lengths`: some decode row has all 2048 positions live.
All inputs are finite; a program needn't handle non-finite values.
Results may differ from the reference program's by a relative error of at most 0.0015.
Values may be sent and summed in bfloat16 or wider, within the bound.
No kernel may reach another device: no remote copies, remote signals or barrier semaphores. Data moves between devices by JAX's collectives and lax.ppermute only.
A program may use at most 128 MiB of HBM per device.

```python
import jax
import jax.numpy as jnp
from jax import lax

DH = 128
KVH = 8
GQ = 8
NEW_DEV = 64
DEC_LEN = 2048
NEW = 2048
CACHED = 32768
ROWS = 128
BLOCKS = 32


def draw_new_queries(key, part):
    key = jax.random.fold_in(key, 11)
    values_in = 3.0 * jax.random.truncated_normal(key, -2.6, 2.6, (NEW, KVH, GQ * DH))
    return values_in.astype(jnp.bfloat16)


def draw_cached_keys(key, part):
    key = jax.random.fold_in(key, 12)
    values_in = jax.random.truncated_normal(key, -6.0, 6.0, (CACHED, KVH, DH))
    return values_in.astype(jnp.bfloat16)


def draw_decode_queries(key, part):
    key = jax.random.fold_in(key, 13)
    values_in = 3.0 * jax.random.truncated_normal(key, -2.6, 2.6, (ROWS, KVH, GQ * DH))
    return values_in.astype(jnp.bfloat16)


def draw_decode_keys(key, part):
    key = jax.random.fold_in(key, 14)
    values_in = jax.random.truncated_normal(key, -6.0, 6.0, (ROWS, DEC_LEN, KVH, DH))
    return values_in.astype(jnp.bfloat16)


def draw_decode_lengths(key, part):
    key = jax.random.fold_in(key, 15)
    lengths_now = jax.random.randint(key, (ROWS,), DEC_LEN // 8, DEC_LEN + 1)
    return lengths_now.at[0].set(DEC_LEN).astype(jnp.int32)


def plant(result, rng, least, high):
    place = [jax.random.randint(jax.random.fold_in(rng, axis), (), 0, length) for axis, length in enumerate(result.shape)]
    longest = result.shape.index(max(result.shape))
    neighbour = place[:longest] + [(place[longest] + 1) % result.shape[longest]] + place[longest + 1:]
    return result.at[tuple(place)].set(least).at[tuple(neighbour)].set(high)


def steps_of(own_key, shape, cuts, least, top_value):
    def one(axis_at, parts):
        heights = jax.random.uniform(jax.random.fold_in(jax.random.fold_in(own_key, 6), axis_at), (parts,), jnp.float32, least / len(cuts), top_value / len(cuts))
        return jnp.repeat(jnp.exp(heights), shape[axis_at] // parts).reshape((-1,) + (1,) * (len(shape) - axis_at - 1))

    factor_of = one(*cuts[0])
    for cut in cuts[1:]:
        factor_of = factor_of * one(*cut)
    return factor_of


def centred(rng, shape, spread, limit, pieces=(), kind=jnp.bfloat16):
    array = spread * jax.random.normal(rng, shape, jnp.float32)
    if pieces:
        array = array * steps_of(rng, shape, pieces, -0.22, 0.18)
    return jnp.clip(array, -limit, limit).astype(kind)


def setup_inputs(seed: int = 0) -> dict:
    key_of = jax.random.split(jax.random.key(seed), 11)
    new_queries = draw_new_queries(jax.random.fold_in(key_of[10], 71), 0)
    new_keys = centred(key_of[1], (NEW, KVH, DH), 1.0, 6.0, ((0, 32), (1, 8)))
    new_values = centred(key_of[2], (NEW, KVH, DH), 1.0, 6.0, ((0, 32), (1, 8)))
    cached_keys = draw_cached_keys(jax.random.fold_in(key_of[10], 71), 0)
    cached_values = centred(key_of[4], (CACHED, KVH, DH), 1.0, 6.0, ((0, 32), (1, 8)))
    decode_queries = draw_decode_queries(jax.random.fold_in(key_of[10], 71), 0)
    decode_keys = draw_decode_keys(jax.random.fold_in(key_of[10], 71), 0)
    decode_values = centred(key_of[7], (ROWS, DEC_LEN, KVH, DH), 1.0, 6.0, ((0, 32), (1, 4), (2, 2)))
    decode_lengths = draw_decode_lengths(jax.random.fold_in(key_of[10], 71), 0)
    source_block = plant(jax.random.randint(key_of[9], (ROWS,), 0, BLOCKS), jax.random.fold_in(key_of[9], 1), 0, BLOCKS - 1).astype(jnp.int32)
    return {"new_queries": new_queries, "new_keys": new_keys, "new_values": new_values, "cached_keys": cached_keys, "cached_values": cached_values, "decode_queries": decode_queries, "decode_keys": decode_keys, "decode_values": decode_values, "decode_lengths": decode_lengths, "source_block": source_block}


neg_fill = -1.0e30


def reference(new_queries, new_keys, new_values, cached_keys, cached_values, decode_queries, decode_keys, decode_values, decode_lengths, source_block):
    scale_factor = DH ** -0.5
    keys_all = jnp.concatenate([cached_keys, new_keys], axis=0)
    values_all = jnp.concatenate([cached_values, new_values], axis=0)
    key_pos = jnp.arange(CACHED + NEW, dtype=jnp.int32)
    query_pos = CACHED + jnp.arange(NEW, dtype=jnp.int32)
    allowed = key_pos[None, :] <= query_pos[:, None]
    head_queries = new_queries.reshape(NEW, KVH * GQ, DH)

    def one_head(head_index):
        kv_head = (head_index // GQ).astype(jnp.int32)
        query_head = lax.dynamic_slice_in_dim(head_queries, head_index, 1, 1)[:, 0]
        key_head = lax.dynamic_slice_in_dim(keys_all, kv_head, 1, 1)[:, 0]
        value_head = lax.dynamic_slice_in_dim(values_all, kv_head, 1, 1)[:, 0]
        scores = jnp.dot(query_head, key_head.T, preferred_element_type=jnp.float32) * scale_factor
        scores = jnp.where(allowed, scores, neg_fill)
        row_max = jnp.max(scores, axis=1, keepdims=True)
        weights = jnp.where(allowed, jnp.exp(scores - row_max), 0.0)
        total_w = jnp.sum(weights, axis=1, keepdims=True)
        summed = jnp.dot(weights, value_head.astype(jnp.float32), precision=lax.Precision.HIGHEST)
        return (summed / total_w).astype(jnp.bfloat16)

    prefill_heads = lax.map(one_head, jnp.arange(KVH * GQ, dtype=jnp.int32))
    prefill_out = prefill_heads.transpose(1, 0, 2).reshape(NEW, KVH, GQ * DH)

    def one_row(row_index):
        cache_k = lax.dynamic_index_in_dim(decode_keys, row_index, 0, keepdims=False)
        cache_v = lax.dynamic_index_in_dim(decode_values, row_index, 0, keepdims=False)
        block_id = lax.dynamic_index_in_dim(source_block, row_index, 0, keepdims=False)
        length_now = lax.dynamic_index_in_dim(decode_lengths, row_index, 0, keepdims=False)
        hand_k = lax.dynamic_slice_in_dim(new_keys, (block_id * NEW_DEV).astype(jnp.int32), NEW_DEV, 0)
        hand_v = lax.dynamic_slice_in_dim(new_values, (block_id * NEW_DEV).astype(jnp.int32), NEW_DEV, 0)
        row_keys = jnp.concatenate([cache_k, hand_k], axis=0).astype(jnp.float32)
        row_values = jnp.concatenate([cache_v, hand_v], axis=0).astype(jnp.float32)
        live_mask = jnp.concatenate([jnp.arange(DEC_LEN, dtype=jnp.int32) < length_now, jnp.ones((NEW_DEV,), dtype=bool)])
        query_row = lax.dynamic_index_in_dim(decode_queries, row_index, 0, keepdims=False)
        query_row = query_row.reshape(KVH, GQ, DH).astype(jnp.float32)
        scores = jnp.einsum('hgd,shd->hgs', query_row, row_keys, precision=lax.Precision.HIGHEST) * scale_factor
        scores = jnp.where(live_mask[None, None, :], scores, neg_fill)
        row_max = jnp.max(scores, axis=2, keepdims=True)
        weights = jnp.where(live_mask[None, None, :], jnp.exp(scores - row_max), 0.0)
        total_w = jnp.sum(weights, axis=2, keepdims=True)
        summed = jnp.einsum('hgs,shd->hgd', weights, row_values, precision=lax.Precision.HIGHEST)
        return (summed / total_w).astype(jnp.bfloat16).reshape(KVH, GQ * DH)

    decode_out = lax.map(one_row, jnp.arange(ROWS, dtype=jnp.int32))
    return prefill_out, decode_out
```

```python
import functools
import math

import jax
import jax.numpy as jnp
from jax import lax
from jax.experimental import pallas as pl
from jax.experimental.pallas import tpu as pltpu
from jax.sharding import PartitionSpec as P

f32 = jnp.float32
bf16 = jnp.bfloat16
i16 = jnp.int16
i32 = jnp.int32

HD = 128
GROUPS = 8
TOK = 64
CACHE = 1024
QS = 8
KS = 4
NEWK = KS * TOK
SCALE2 = HD**-0.5 * math.log2(math.e)
NEG = -1e30
NOTHING = -1000.0
CODE = 32767.0
MESSAGE = 144
VMEM_LIMIT = 56 * 2**20


def contract_last(a, b):
    return lax.dot_general(a, b, (((1,), (1,)), ((), ())), preferred_element_type=f32)


def matmul(a, b):
    return jnp.dot(a, b, preferred_element_type=f32)


def split(p):
    high = p.astype(bf16)
    return high, (p - high.astype(f32)).astype(bf16)


def two_words(x):
    big = jnp.round(x * 32.0)
    return big, jnp.round((x * 32.0 - big) * 32768.0)


def one_number(big, small):
    return (big + small * (1.0 / 32768.0)) * (1.0 / 32.0)


def prefill_kernel(*refs):
    meta = refs[0]
    queries = refs[1 : 1 + QS]
    pairs = refs[1 + QS : 1 + QS + KS]
    outs = refs[1 + QS + KS : 1 + 2 * QS + KS]
    q_all, new_keys, values_t, out_t, lse_all = refs[1 + 2 * QS + KS :]
    for s in range(QS):
        q_all[s] = queries[s][...]
    for j in range(KS):
        new_keys[j * TOK : (j + 1) * TOK, :] = pairs[j][CACHE : CACHE + TOK, :]
        values_t[:, j * CACHE : (j + 1) * CACHE] = pairs[j][CACHE + TOK : 2 * CACHE + TOK, :].T
    new_values = jnp.concatenate([pairs[j][2 * CACHE + TOK :, :] for j in range(KS)], 0)
    values_t[:, KS * CACHE :] = new_values.T

    def keys_of(i):
        return pairs[i][:CACHE, :] if i < KS else new_keys[...]

    def values_of(i):
        return values_t[:, i * CACHE : min((i + 1) * CACHE, KS * CACHE + NEWK)]

    def tile_queries(b, half):
        start = half * (4 * HD)
        return jnp.concatenate(
            [q_all[b, :, start + g * HD : start + (g + 1) * HD] for g in range(4)], 0
        )

    def allowed(b):
        offset = lax.broadcasted_iota(i32, (TOK, 4 * TOK), 0)
        token = lax.broadcasted_iota(i32, (TOK, 4 * TOK), 1) & (TOK - 1)
        limit = token + meta[b] * TOK
        return jnp.concatenate(
            [offset + meta[QS + j] * TOK <= limit for j in range(KS)], 0
        )

    def put(b, half, total, acc):
        lanes = slice(half * 4 * TOK, (half + 1) * 4 * TOK)
        out_t[b, :, lanes] = acc / total
        lse_all[b, 0:1, lanes] = jnp.log2(total)

    def one_block(b, carry):
        mask = allowed(b)
        tiles = [tile_queries(b, half) for half in range(2)]
        sums = [jnp.zeros((8, 4 * TOK), f32) for unused in range(2)]
        accs = [jnp.zeros((HD, 4 * TOK), f32) for unused in range(2)]
        work = [(i, t) for i in range(KS + 1) for t in range(2)]
        following = contract_last(keys_of(0), tiles[0])
        for w, (i, t) in enumerate(work):
            scores = following
            if w + 1 < len(work):
                following = contract_last(keys_of(work[w + 1][0]), tiles[work[w + 1][1]])
            weights = jnp.exp2(scores * SCALE2)
            if i == KS:
                weights = jnp.where(mask, weights, 0.0)
            sums[t] = sums[t] + jnp.sum(weights.reshape(-1, 8, 4 * TOK), 0)
            high, low = split(weights)
            accs[t] = accs[t] + matmul(values_of(i), high) + matmul(values_of(i), low)
        for t in range(2):
            put(b, t, jnp.sum(sums[t], 0, keepdims=True), accs[t])
        return carry

    lax.fori_loop(0, QS, one_block, 0)

    lse = lse_all[:, 0, :]
    fine = jnp.where((lse > -60.0) & (lse < 100.0), 0, 1)

    @pl.when(jnp.max(fine) > 0)
    def again():
        def one(b, carry):
            mask = allowed(b)
            for t in range(2):
                tile = tile_queries(b, t)
                top = jnp.full((1, 4 * TOK), NEG, f32)
                total = jnp.zeros((1, 4 * TOK), f32)
                acc = jnp.zeros((HD, 4 * TOK), f32)
                for i in range(KS + 1):
                    scores = contract_last(keys_of(i), tile) * SCALE2
                    if i == KS:
                        scores = jnp.where(mask, scores, NEG)
                    new_top = jnp.maximum(top, jnp.max(scores, 0, keepdims=True))
                    weights = jnp.exp2(scores - new_top)
                    factor = jnp.exp2(top - new_top)
                    total = total * factor + jnp.sum(weights, 0, keepdims=True)
                    high, low = split(weights)
                    acc = acc * factor + matmul(values_of(i), high) + matmul(values_of(i), low)
                    top = new_top
                put(b, t, total, acc)
                lanes = slice(t * 4 * TOK, (t + 1) * 4 * TOK)
                lse_all[b, 0:1, lanes] = jnp.log2(total) + top
            return carry

        lax.fori_loop(0, QS, one, 0)

    hand_q = jnp.concatenate([q_all[s, 0:32, 8 * HD :] for s in range(QS)], 0)
    source = jnp.concatenate([q_all[s, 32:64, 8 * HD :] for s in range(QS)], 0).astype(f32)
    lane = lax.broadcasted_iota(i32, (QS * 32, HD), 1)
    keep = jnp.concatenate(
        [
            source == jnp.where(lane < TOK, meta[QS + 2 * j], meta[QS + 2 * j + 1]).astype(f32)
            for j in range(2)
        ],
        1,
    )
    scores = jnp.where(keep, contract_last(hand_q, new_keys[...]) * SCALE2, NEG)
    top = jnp.max(scores, 1, keepdims=True)
    weights = jnp.where(keep, jnp.exp2(scores - top), 0.0)
    total = jnp.sum(weights, 1, keepdims=True)
    both = matmul(jnp.concatenate(split(weights), 0), new_values)
    some = total > 0.0
    hand = (both[: QS * 32] + both[QS * 32 :]) / jnp.where(some, total, 1.0)
    hand_lse = jnp.where(some, jnp.log2(jnp.where(some, total, 1.0)) + top, NOTHING)
    most = jnp.maximum(jnp.max(jnp.abs(hand), 1, keepdims=True), 1e-30)
    hand = hand * (CODE / most)
    wide_lse = jnp.broadcast_to(hand_lse, (QS * 32, HD))
    wide_most = jnp.broadcast_to(jnp.log2(most), (QS * 32, HD))
    row_lse = jnp.concatenate([wide_lse[:HD].T[0:8], wide_lse[HD:].T[0:8]], 1)
    row_most = jnp.concatenate([wide_most[:HD].T[0:8], wide_most[HD:].T[0:8]], 1)

    for s in range(QS):
        out = out_t[s]
        most_t = jnp.maximum(jnp.max(jnp.abs(out), 0, keepdims=True), 1e-30)
        outs[s][0:HD, :] = jnp.round(out * (CODE / most_t)).astype(i32).astype(i16)
        lse_words = two_words(lse_all[s, 0:1, :])
        most_words = two_words(jnp.log2(most_t))
        spare = jnp.zeros((1, 8 * TOK - 32), f32)
        lanes = slice(s * 32, (s + 1) * 32)
        small = [jnp.concatenate([row[0:1, lanes], spare], 1) for row in (row_lse, row_most)]
        words = [*two_words(small[0]), *two_words(small[1])]
        slab = jnp.concatenate([hand[s * 32 + 8 * k : s * 32 + 8 * k + 8] for k in range(4)], 1)
        rest = jnp.concatenate([*lse_words, *most_words, *words, jnp.round(slab)], 0)
        outs[s][HD:MESSAGE, :] = rest.astype(i32).astype(i16)


def prefill(meta, queries, pairs):
    vmem = pl.BlockSpec(memory_space=pltpu.VMEM)
    return pl.pallas_call(
        prefill_kernel,
        name="prefill",
        in_specs=[pl.BlockSpec(memory_space=pltpu.SMEM)] + [vmem] * (QS + KS),
        out_specs=[vmem] * QS,
        out_shape=[jax.ShapeDtypeStruct((MESSAGE, 8 * TOK), i16)] * QS,
        scratch_shapes=[
            pltpu.VMEM((QS, TOK, 9 * HD), bf16),
            pltpu.VMEM((NEWK, HD), bf16),
            pltpu.VMEM((HD, KS * CACHE + NEWK), bf16),
            pltpu.VMEM((QS, HD, 8 * TOK), f32),
            pltpu.VMEM((QS, 8, 8 * TOK), f32),
        ],
        compiler_params=pltpu.CompilerParams(vmem_limit_bytes=VMEM_LIMIT),
        cost_estimate=pl.CostEstimate(
            flops=6 * 4096 * 4352 * 128 * 2, bytes_accessed=4_000_000, transcendentals=4096 * 4352
        ),
    )(meta, *queries, *pairs)


def combine_kernel(*refs):
    parts = refs[:QS]
    out_ref, hand_ref = refs[QS:]
    tails = [part[HD:MESSAGE, :].astype(i32).astype(f32) for part in parts]
    lse = [one_number(tail[0:1], tail[1:2]) for tail in tails]
    most = [one_number(tail[2:3], tail[3:4]) for tail in tails]
    top = functools.reduce(jnp.maximum, lse)
    total = sum(jnp.exp2(x - top) for x in lse)
    acc = jnp.zeros((HD, 8 * TOK), f32)
    for s in range(QS):
        factor = jnp.exp2(lse[s] + most[s] - top) / (total * CODE)
        acc = acc + parts[s][0:HD, :].astype(i32).astype(f32) * factor
    rows = acc.T
    for g in range(GROUPS):
        out_ref[:, g * HD : (g + 1) * HD] = rows[g * TOK : (g + 1) * TOK].astype(bf16)
    small = jnp.concatenate(
        [tail[4:8, 0:HD] for tail in tails] + [jnp.zeros((HD - 4 * QS, HD), f32)], 0
    )
    columns = small.T[0:32]
    lse, most = [], []
    for s in range(QS):
        four = [columns[:, 4 * s + k : 4 * s + k + 1] for k in range(4)]
        lse.append(one_number(four[0], four[1]))
        most.append(one_number(four[2], four[3]))
    top = functools.reduce(jnp.maximum, lse)
    total = sum(jnp.exp2(x - top) for x in lse)
    hand = jnp.zeros((32, HD), f32)
    for s in range(QS):
        slab = jnp.concatenate([tails[s][8:16, k * HD : (k + 1) * HD] for k in range(4)], 0)
        hand = hand + slab * (jnp.exp2(lse[s] + most[s] - top) / (total * CODE))
    hand_ref[0:32] = hand
    hand_ref[32:64] = jnp.broadcast_to(jnp.log2(total) + top, (32, HD))


def combine(parts):
    return pl.pallas_call(
        combine_kernel,
        name="combine",
        out_shape=[
            jax.ShapeDtypeStruct((TOK, 8 * HD), bf16),
            jax.ShapeDtypeStruct((64, HD), f32),
        ],
        compiler_params=pltpu.CompilerParams(vmem_limit_bytes=VMEM_LIMIT),
        cost_estimate=pl.CostEstimate(flops=2_000_000, bytes_accessed=1_300_000, transcendentals=10_000),
    )(*parts)


def decode_kernel(meta, q_ref, k_ref, v_ref, out_ref):
    row = pl.program_id(0)
    scores = contract_last(q_ref[0], k_ref[0]) * SCALE2
    column = lax.broadcasted_iota(i32, scores.shape, 1)
    head = lax.broadcasted_iota(i32, scores.shape, 0) >> 3
    keep = ((column & 3) == head) & ((column >> 2) < meta[row])
    scores = jnp.where(keep, scores, NEG)
    top = jnp.max(scores, 1, keepdims=True)
    weights = jnp.where(keep, jnp.exp2(scores - top), 0.0)
    total = jnp.sum(weights, 1, keepdims=True)
    both = matmul(jnp.concatenate(split(weights), 0), v_ref[0])
    some = total > 0.0
    safe = jnp.where(some, total, 1.0)
    out_ref[0, 0:32] = (both[0:32] + both[32:64]) / safe
    out_ref[0, 32:64] = jnp.broadcast_to(
        jnp.where(some, jnp.log2(safe) + top, NOTHING), (32, HD)
    )


def decode_cache(live, queries, keys, values):
    rows, width, unused = keys.shape
    return pl.pallas_call(
        decode_kernel,
        name="decode_cache",
        grid=(rows,),
        in_specs=[
            pl.BlockSpec(memory_space=pltpu.SMEM),
            pl.BlockSpec((1, 32, HD), lambda r: (r, 0, 0)),
            pl.BlockSpec((1, width, HD), lambda r: (r, 0, 0)),
            pl.BlockSpec((1, width, HD), lambda r: (r, 0, 0)),
        ],
        out_specs=pl.BlockSpec((1, 64, HD), lambda r: (r, 0, 0)),
        out_shape=jax.ShapeDtypeStruct((rows, 64, HD), f32),
        compiler_params=pltpu.CompilerParams(vmem_limit_bytes=VMEM_LIMIT),
        cost_estimate=pl.CostEstimate(
            flops=200_000_000, bytes_accessed=4_400_000, transcendentals=262_144
        ),
    )(live, queries, keys, values)


def finish_kernel(*refs):
    meta = refs[0]
    parts = refs[1:5]
    hands = refs[5:9]
    out_ref, placed = refs[9:]
    for k in range(4):
        placed[meta[k]] = hands[k][...]
    for r in range(4):
        rows = slice(r * 8, r * 8 + 8)
        outs = [part[r, 0:32] for part in parts]
        lse = [part[r, 32:64] for part in parts]
        outs.append(jnp.concatenate([placed[j, rows] for j in range(4)], 0))
        lse.append(jnp.concatenate([placed[j, r * 8 + 32 : r * 8 + 40] for j in range(4)], 0))
        top = functools.reduce(jnp.maximum, lse)
        factors = [jnp.exp2(x - top) for x in lse]
        out_ref[r] = (sum(o * w for o, w in zip(outs, factors)) / sum(factors)).astype(bf16)


def finish(meta, parts, hands):
    vmem = pl.BlockSpec(memory_space=pltpu.VMEM)
    return pl.pallas_call(
        finish_kernel,
        name="finish",
        in_specs=[pl.BlockSpec(memory_space=pltpu.SMEM)] + [vmem] * 8,
        out_specs=vmem,
        out_shape=jax.ShapeDtypeStruct((4, 32, HD), bf16),
        scratch_shapes=[pltpu.VMEM((4, 64, HD), f32)],
    )(meta, *parts, *hands)


def local(
    new_queries,
    new_keys,
    new_values,
    cached_keys,
    cached_values,
    decode_queries,
    decode_keys,
    decode_values,
    decode_lengths,
    source_block,
):
    ctx = lax.axis_index("ctx")
    tp = lax.axis_index("tp")
    grp = lax.axis_index("grp")
    count = lax.axis_size("ctx")

    def swap(x, bits):
        return lax.ppermute(x, "ctx", [(i, i ^ bits) for i in range(count)])

    pair = jnp.concatenate(
        [cached_keys[:, 0], new_keys[:, 0], cached_values[:, 0], new_values[:, 0]], 0
    )
    pairs = [pair] + [swap(pair, j) for j in (1, 3, 2)]
    pairs = [pairs[0], pairs[1], pairs[3], pairs[2]]

    own_place = 2 * (tp & 1) + grp
    other_place = 2 * (tp & 1) + 1 - grp
    mine = lax.dynamic_index_in_dim(decode_queries, own_place, 1, False)
    theirs = lax.dynamic_index_in_dim(decode_queries, other_place, 1, False)
    got = lax.ppermute(theirs, "grp", [(0, 1), (1, 0)])
    hand_q = jnp.where(grp == (tp >> 1), mine, got).reshape(32, HD)
    source = jnp.broadcast_to(jnp.repeat(source_block.astype(bf16), 8)[:, None], (32, HD))
    query = jnp.concatenate([new_queries[:, 0], jnp.concatenate([hand_q, source], 0)], 1)
    queries = [query] + [swap(query, s << 2) for s in range(1, QS)]

    width = decode_keys.shape[1]
    live = decode_lengths - tp * width
    part = decode_cache(
        live,
        decode_queries.reshape(4, 32, HD),
        decode_keys.reshape(4, width * 4, HD),
        decode_values.reshape(4, width * 4, HD),
    )
    parts = [part] + [
        lax.ppermute(part, "tp", [(i, (i + k) % 4) for i in range(4)]) for k in range(1, 4)
    ]

    slots = [s << 2 for s in range(QS)] + list(range(KS))
    messages = prefill(ctx ^ jnp.array(slots, i32), queries, pairs)
    returned = [messages[0]] + [swap(messages[s], s << 2) for s in range(1, QS)]
    prefill_out, hand = combine(returned)

    def round_of(k):
        pairs_of = []
        for t in range(4):
            for g in range(2):
                to = ((t % 2) * 2 + g + k) % 4
                pairs_of.append((t * 2 + g, to * 2 + t // 2))
        return lax.ppermute(hand, ("tp", "grp"), pairs_of)

    hands = [round_of(k) for k in range(4)]
    places = (tp - jnp.arange(4, dtype=i32)) & 3
    decode_out = finish(places, parts, hands)
    return (prefill_out[:, None, :], decode_out.reshape(4, 4, 8 * HD))


def solution(mesh):
    in_specs = (
        P("ctx", ("tp", "grp"), None),
        P("ctx", ("tp", "grp"), None),
        P("ctx", ("tp", "grp"), None),
        P("ctx", ("tp", "grp"), None),
        P("ctx", ("tp", "grp"), None),
        P("ctx", "grp", None),
        P("ctx", "tp", "grp", None),
        P("ctx", "tp", "grp", None),
        P("ctx"),
        P("ctx"),
    )
    out_specs = (P("ctx", ("tp", "grp"), None), P("ctx", "grp", None))
    return jax.shard_map(local, mesh=mesh, in_specs=in_specs, out_specs=out_specs, check_vma=False)
```

```python
import functools
import math

import jax
import jax.numpy as jnp
from jax import lax
from jax.experimental import pallas as pl
from jax.experimental.pallas import tpu as pltpu
from jax.sharding import PartitionSpec as P

f32 = jnp.float32
bf16 = jnp.bfloat16
i16 = jnp.int16
i32 = jnp.int32

HD = 128
GROUPS = 8
TOK = 64
CACHE = 1024
QS = 8
KS = 4
NEWK = KS * TOK
TILE = 4 * TOK
SCALE2 = HD**-0.5 * math.log2(math.e)
NEG = -1e30
NOTHING = -1000.0
CODE = 32767.0
FIRST = 176
SECOND = 144
EARLY = 3
VMEM_LIMIT = 20 * 2**20
VMEM = pl.BlockSpec(memory_space=pltpu.VMEM)
SMEM = pl.BlockSpec(memory_space=pltpu.SMEM)


def contract_last(a, b):
    return lax.dot_general(a, b, (((1,), (1,)), ((), ())), preferred_element_type=f32)


def matmul(a, b):
    return jnp.dot(a, b, preferred_element_type=f32)


def split(p):
    high = p.astype(bf16)
    return high, (p - high.astype(f32)).astype(bf16)


def two_words(x):
    big = jnp.round(x * 32.0)
    return big, jnp.round((x * 32.0 - big) * 32768.0)


def one_number(big, small):
    return (big + small * (1.0 / 32768.0)) * (1.0 / 32.0)


def call(
    kernel, name, outs, count, scratch=(), cost=(1_000_000, 500_000, 1000), vmem=VMEM_LIMIT, **kwargs
):
    return pl.pallas_call(
        kernel,
        name=name,
        out_shape=outs,
        scratch_shapes=scratch,
        compiler_params=pltpu.CompilerParams(vmem_limit_bytes=vmem),
        cost_estimate=pl.CostEstimate(
            flops=cost[0], bytes_accessed=cost[1], transcendentals=cost[2]
        ),
        **kwargs,
    )


def keys_of(pair):
    return pair[0:CACHE, :]


def values_of(pair):
    return pair[CACHE : 2 * CACHE, :].T


def new_of(pairs, which):
    start = 2 * CACHE + which * TOK
    return jnp.concatenate([ref[start : start + TOK, :] for ref in pairs], 0)


def pack_query_kernel(meta, source, new_queries, dec_queries, out, rows):
    upper = meta[0] > 0
    mine, blocks = [], []
    for r in range(4):
        wide = dec_queries[r].astype(f32)
        heads = [
            jnp.concatenate([wide[j : j + 1, g * HD : (g + 1) * HD] for g in range(GROUPS)], 0)
            for j in range(4)
        ]
        rows[r] = jnp.concatenate(heads, 0).astype(bf16)
        mine += [jnp.where(upper, heads[2 + j], heads[j]) for j in range(2)]
        block = jnp.where(meta[1] > 0, source[r], -1).astype(f32)
        blocks.append(jnp.full((16, HD), block, f32).astype(bf16))
    mine = jnp.concatenate(mine, 0).astype(bf16)
    blocks = jnp.concatenate(blocks, 0)
    for s in range(QS):
        out[s, :, 0 : 8 * HD] = new_queries[...]
        out[s, :, 8 * HD : 9 * HD] = mine
        out[s, :, 9 * HD :] = blocks


def tile_queries(queries, b, half):
    start = half * (4 * HD)
    return jnp.concatenate(
        [queries[b, :, start + g * HD : start + (g + 1) * HD] for g in range(4)], 0
    )


def accumulate(tiles, states, blocks):
    work = [(i, t) for i in range(len(blocks)) for t in range(len(tiles))]
    states = list(states)
    following = contract_last(blocks[0][0](), tiles[0])
    for w, (i, t) in enumerate(work):
        scores = following
        if w + 1 < len(work):
            following = contract_last(blocks[work[w + 1][0]][0](), tiles[work[w + 1][1]])
        weights = jnp.exp2(scores * SCALE2)
        if blocks[i][2] is not None:
            weights = jnp.where(blocks[i][2][t], weights, 0.0)
        total, acc = states[t]
        total = total + jnp.sum(weights.reshape(-1, 8, TILE), 0)
        high, low = split(weights)
        values = blocks[i][1]()
        states[t] = (total, acc + matmul(values, high) + matmul(values, low))
    return states


def hand_off(meta, queries, pairs, out):
    rows = QS * 32
    lane = lax.broadcasted_iota(i32, (rows, HD), 1)
    pieces = [(s, r * 16) for s in range(QS) for r in range(4)]
    all_q = [queries[s, :, 8 * HD : 9 * HD].astype(f32) for s in range(QS)]
    all_source = [queries[s, :, 9 * HD :].astype(f32) for s in range(QS)]
    source = jnp.concatenate([all_source[s][a : a + 8] for s, a in pieces], 0)
    keep = jnp.concatenate(
        [
            source == jnp.where(lane < TOK, meta[QS + 2 * j], meta[QS + 2 * j + 1]).astype(f32)
            for j in range(2)
        ],
        1,
    )
    own = meta[QS + KS]
    results = []
    for head in range(2):
        hand_q = jnp.concatenate(
            [all_q[s][a + 8 * head : a + 8 * head + 8] for s, a in pieces], 0
        ).astype(bf16)
        keys = jnp.where(own == head, new_of(pairs, 0), new_of(pairs, 2))
        values = jnp.where(own == head, new_of(pairs, 1), new_of(pairs, 3))
        scores = jnp.where(keep, contract_last(hand_q, keys) * SCALE2, NEG)
        top = jnp.max(scores, 1, keepdims=True)
        weights = jnp.where(keep, jnp.exp2(scores - top), 0.0)
        total = jnp.sum(weights, 1, keepdims=True)
        both = matmul(jnp.concatenate(split(weights), 0), values)
        some = total > 0.0
        safe = jnp.where(some, total, 1.0)
        hand = (both[:rows] + both[rows:]) / safe
        lse = jnp.where(some, jnp.log2(safe) + top, NOTHING)
        most = jnp.maximum(jnp.max(jnp.abs(hand), 1, keepdims=True), 1e-30)
        hand = jnp.round(hand * (CODE / most))
        wide = [jnp.broadcast_to(x, (rows, HD)) for x in (lse, jnp.log2(most))]
        results.append((hand, [[x[:HD].T[0:1], x[HD:].T[0:1]] for x in wide]))
    sums = []
    for s in range(QS):
        slabs = [results[head][0][s * 32 : s * 32 + 32] for head in range(2)]
        out[s, HD + 16 : FIRST, :] = jnp.concatenate(slabs, 1).astype(i32).astype(i16)
        words = []
        for kind in range(2):
            place = s * 32 % HD
            pieces = [results[head][1][kind][s // 4][:, place : place + 32] for head in range(2)]
            row = jnp.concatenate(pieces + [jnp.zeros((1, TILE - 64), f32)], 1)
            words += [*two_words(row)]
        sums.append(words)
    return sums


def prefill_early_kernel(queries, *refs):
    pairs, (acc0, acc1, sum0, sum1, values_t) = refs[:EARLY], refs[EARLY:]
    for j, pair in enumerate(pairs):
        values_t[j] = values_of(pair)
    blocks = [
        (functools.partial(keys_of, pairs[j]), lambda j=j: values_t[j], None) for j in range(EARLY)
    ]

    def step(b, carry):
        tiles = [tile_queries(queries, b, half) for half in range(2)]
        zero = (jnp.zeros((8, TILE), f32), jnp.zeros((HD, TILE), f32))
        states = accumulate(tiles, [zero, zero], blocks)
        (sum0[b], acc0[b]), (sum1[b], acc1[b]) = states
        return carry

    lax.fori_loop(0, QS, step, 0)


def prefill_early(queries, pairs):
    outs = [jax.ShapeDtypeStruct((QS, HD, TILE), f32)] * 2
    outs += [jax.ShapeDtypeStruct((QS, 8, TILE), f32)] * 2
    return call(
        prefill_early_kernel, "prefill_early", outs, 1 + EARLY,
        scratch=[pltpu.VMEM((EARLY, HD, CACHE), bf16)],
        cost=(6 * 4096 * 1024 * EARLY * 128, 4_000_000, 4096 * 1024 * EARLY),
    )(queries, *pairs)


def prefill_late_kernel(half, meta, queries, *refs):
    pairs = refs[:KS]
    acc_in, sum_in, out, out_t, lse_all, values_t = refs[KS:]
    new_keys = new_of(pairs, 0)
    new_values_t = new_of(pairs, 1).T
    for j in range(EARLY, KS):
        values_t[j - EARLY] = values_of(pairs[j])
    cached = [
        (functools.partial(keys_of, pairs[j]), lambda j=j: values_t[j - EARLY], None)
        for j in range(EARLY, KS)
    ]

    def allowed(b):
        offset = lax.broadcasted_iota(i32, (TOK, TILE), 0)
        token = lax.broadcasted_iota(i32, (TOK, TILE), 1) & (TOK - 1)
        limit = token + meta[b] * TOK
        return jnp.concatenate([offset + meta[QS + j] * TOK <= limit for j in range(KS)], 0)

    def step(n, carry):
        places = [4 * n + k for k in range(4)]
        tiles = [tile_queries(queries, b, half) for b in places]
        new = (lambda: new_keys, lambda: new_values_t, [allowed(b) for b in places])
        states = [(sum_in[b], acc_in[b]) for b in places]
        for b, (total, acc) in zip(places, accumulate(tiles, states, cached + [new])):
            total = jnp.sum(total, 0, keepdims=True)
            out_t[b] = acc / total
            lse_all[b] = jnp.log2(total)
        return carry

    lax.fori_loop(0, QS // 4, step, 0)

    lse = lse_all[:, 0, :]
    outside = jnp.where((lse > -60.0) & (lse < 100.0), 0, 1)

    @pl.when(jnp.max(outside) > 0)
    def again():
        blocks = [
            (functools.partial(keys_of, pair), functools.partial(values_of, pair)) for pair in pairs
        ]
        blocks.append((lambda: new_keys, lambda: new_values_t))

        def one(b, carry):
            mask = allowed(b)
            tile = tile_queries(queries, b, half)
            top = jnp.full((1, TILE), NEG, f32)
            total = jnp.zeros((1, TILE), f32)
            acc = jnp.zeros((HD, TILE), f32)
            for i, block in enumerate(blocks):
                scores = contract_last(block[0](), tile) * SCALE2
                if i == KS:
                    scores = jnp.where(mask, scores, NEG)
                new_top = jnp.maximum(top, jnp.max(scores, 0, keepdims=True))
                weights = jnp.exp2(scores - new_top)
                factor = jnp.exp2(top - new_top)
                total = total * factor + jnp.sum(weights, 0, keepdims=True)
                first, second = split(weights)
                values = block[1]()
                acc = acc * factor + matmul(values, first) + matmul(values, second)
                top = new_top
            out_t[b] = acc / total
            lse_all[b] = jnp.log2(total) + top
            return carry

        lax.fori_loop(0, QS, one, 0)

    if half == 0:
        hand_sums = hand_off(meta, queries, pairs, out)
    for s in range(QS):
        result = out_t[s]
        most = jnp.maximum(jnp.max(jnp.abs(result), 0, keepdims=True), 1e-30)
        out[s, 0:HD, :] = jnp.round(result * (CODE / most)).astype(i32).astype(i16)
        words = [*two_words(lse_all[s]), *two_words(jnp.log2(most))]
        words += hand_sums[s] if half == 0 else []
        words += [jnp.zeros((16 - len(words), TILE), f32)]
        out[s, HD : HD + 16, :] = jnp.concatenate(words, 0).astype(i32).astype(i16)


def prefill_late(half, meta, queries, pairs, acc, total):
    return call(
        functools.partial(prefill_late_kernel, half),
        "prefill_second" if half else "prefill_first",
        jax.ShapeDtypeStruct((QS, SECOND if half else FIRST, TILE), i16), 8,
        scratch=[
            pltpu.VMEM((QS, HD, TILE), f32),
            pltpu.VMEM((QS, 1, TILE), f32),
            pltpu.VMEM((KS - EARLY, HD, CACHE), bf16),
        ],
        in_specs=[SMEM] + [VMEM] * 7,
        out_specs=VMEM,
        cost=(6 * 2048 * 1280 * 128, 4_000_000, 2048 * 1280),
    )(meta, queries, *pairs, acc, total)


def merge(outs, lses):
    top = functools.reduce(jnp.maximum, lses)
    factors = [jnp.exp2(x - top) for x in lses]
    total = sum(factors)
    return sum(o * w for o, w in zip(outs, factors)) / total, jnp.log2(total) + top


def combine_kernel(first, second, out):
    for half, parts in enumerate((first, second)):
        tails = [parts[s, HD : HD + 16, :].astype(i32).astype(f32) for s in range(QS)]
        lse = [one_number(tail[0:1], tail[1:2]) for tail in tails]
        most = [one_number(tail[2:3], tail[3:4]) for tail in tails]
        top = functools.reduce(jnp.maximum, lse)
        total = sum(jnp.exp2(x - top) for x in lse) * CODE
        acc = jnp.zeros((HD, TILE), f32)
        for s in range(QS):
            factor = jnp.exp2(lse[s] + most[s] - top) / total
            acc = acc + parts[s, 0:HD, :].astype(i32).astype(f32) * factor
        rows = acc.T
        for g in range(4):
            lanes = slice((half * 4 + g) * HD, (half * 4 + g + 1) * HD)
            out[:, lanes] = rows[g * TOK : (g + 1) * TOK].astype(bf16)


def as_row(wide):
    return wide.T[0:8]


def as_columns(row):
    return jnp.broadcast_to(row[0:1], (HD, HD)).T


def decode_kernel(meta, q_ref, k_ref, v_ref, out_ref, lse_ref):
    row = pl.program_id(0)
    scores = contract_last(q_ref[0], k_ref[0]) * SCALE2
    column = lax.broadcasted_iota(i32, scores.shape, 1)
    head = lax.broadcasted_iota(i32, scores.shape, 0) >> 3
    keep = ((column & 3) == head) & ((column >> 2) < meta[row])
    scores = jnp.where(keep, scores, NEG)
    top = jnp.max(scores, 1, keepdims=True)
    weights = jnp.where(keep, jnp.exp2(scores - top), 0.0)
    total = jnp.sum(weights, 1, keepdims=True)
    both = matmul(jnp.concatenate(split(weights), 0), v_ref[0])
    some = total > 0.0
    safe = jnp.where(some, total, 1.0)
    place = pl.ds(pl.multiple_of(row * 32, 32), 32)
    out_ref[place, :] = (both[0:32] + both[32:64]) / safe
    lse_ref[place, :] = jnp.broadcast_to(jnp.where(some, jnp.log2(safe) + top, NOTHING), (32, HD))

    @pl.when(row == 3)
    def last():
        out_ref[HD:, :] = as_row(lse_ref[...])


def decode_cache(live, queries, keys, values):
    rows, width, unused = keys.shape
    return call(
        decode_kernel, "decode_cache", jax.ShapeDtypeStruct((HD + 8, HD), f32), 4,
        scratch=[pltpu.VMEM((HD, HD), f32)],
        cost=(2_000_000_000, 4_400_000, 262_144),
        grid=(rows,),
        in_specs=[
            SMEM,
            pl.BlockSpec((1, 32, HD), lambda r: (r, 0, 0)),
            pl.BlockSpec((1, width, HD), lambda r: (r, 0, 0)),
            pl.BlockSpec((1, width, HD), lambda r: (r, 0, 0)),
        ],
        out_specs=pl.BlockSpec((HD + 8, HD), lambda r: (0, 0)),
    )(live, queries, keys, values)


def merge_hand_kernel(meta, part, back, out):
    tails = [back[s, HD : HD + 16, :].astype(i32).astype(f32)[4:8, 0:HD] for s in range(QS)]
    columns = jnp.concatenate(tails + [jnp.zeros((HD - 4 * QS, HD), f32)], 0).T
    slabs = [back[s, HD + 16 : FIRST, :].astype(i32).astype(f32) for s in range(QS)]
    heads = []
    for head in range(2):
        outs, sums = [], []
        for s in range(QS):
            four = [
                columns[head * 32 : head * 32 + 32, 4 * s + k : 4 * s + k + 1] for k in range(4)
            ]
            sums.append(one_number(four[0], four[1]))
            scale = jnp.exp2(one_number(four[2], four[3])) / CODE
            outs.append(slabs[s][:, head * HD : (head + 1) * HD] * scale)
        result, lse = merge(outs, sums)
        heads.append((result, jnp.broadcast_to(lse, (32, HD))))
    upper = meta[0] > 0
    blocks, lses = [], []
    for r in range(4):
        for j in range(4):
            fits = upper if j >= 2 else jnp.logical_not(upper)
            result, lse = (x[r * 8 : r * 8 + 8] for x in heads[j % 2])
            blocks.append(jnp.where(fits, result, 0.0))
            lses.append(jnp.where(fits, lse, NOTHING))
    result, lse = merge(
        [part[0:HD], jnp.concatenate(blocks, 0)],
        [as_columns(part[HD:]), jnp.concatenate(lses, 0)],
    )
    most = jnp.maximum(jnp.max(jnp.abs(result), 1, keepdims=True), 1e-30)
    out[0:HD] = jnp.round(result * (CODE / most)).astype(i32).astype(i16)
    wide = jnp.broadcast_to(jnp.log2(most), (HD, HD))
    words = [*two_words(as_row(lse)[0:1]), *two_words(as_row(wide)[0:1]), jnp.zeros((12, HD), f32)]
    out[HD:] = jnp.concatenate(words, 0).astype(i32).astype(i16)


def finish_kernel(meta, *refs):
    parts, (out, placed, rows) = refs[:4], refs[4:]
    for k in range(4):
        placed[meta[2] ^ k] = parts[k][...]
    tails = [placed[t, HD:].astype(i32).astype(f32) for t in range(4)]
    columns = jnp.concatenate(tails + [jnp.zeros((HD - 64, HD), f32)], 0).T
    outs, lses = [], []
    for t in range(4):
        four = [columns[:, 16 * t + k : 16 * t + k + 1] for k in range(4)]
        lses.append(one_number(four[0], four[1]))
        scale = jnp.exp2(one_number(four[2], four[3])) / CODE
        outs.append(placed[t, 0:HD].astype(i32).astype(f32) * scale)
    rows[...] = merge(outs, lses)[0]
    for r in range(4):
        for g in range(GROUPS):
            lanes = slice(g * HD, (g + 1) * HD)
            out[r, :, lanes] = rows[pl.ds(r * 32 + g, 4, stride=8), :].astype(bf16)


def local(
    new_queries,
    new_keys,
    new_values,
    cached_keys,
    cached_values,
    decode_queries,
    decode_keys,
    decode_values,
    decode_lengths,
    source_block,
):
    ctx = lax.axis_index("ctx")
    tp = lax.axis_index("tp")
    grp = lax.axis_index("grp")
    count = lax.axis_size("ctx")
    struct = jax.ShapeDtypeStruct

    def exchange(x):
        groups = [
            [z + 4 * (k >> 1) + y + (k & 1) for k in range(QS)] for z in (0, 16) for y in (0, 2)
        ]
        return lax.all_to_all(x, "ctx", 0, 0, axis_index_groups=groups, tiled=True)

    def other_core(x):
        return lax.ppermute(x, "grp", [(0, 1), (1, 0)])

    own_new = (new_keys[:, 0], new_values[:, 0])
    pair = jnp.concatenate(
        [cached_keys[:, 0], cached_values[:, 0], *own_new, *[other_core(x) for x in own_new]], 0
    )

    def swap(x, bits):
        return lax.ppermute(x, "ctx", [(i, i ^ bits) for i in range(count)])

    sent = [swap(pair, 16), swap(pair, 3)]

    holds = (grp == (tp >> 1)).astype(i32)
    flags = jnp.stack([tp & 1, holds, tp]).astype(i32)
    query, dec_queries = call(
        pack_query_kernel, "pack_query",
        [struct((QS, TOK, 10 * HD), bf16), struct((4, 32, HD), bf16)], 4,
        in_specs=[SMEM] * 2 + [VMEM] * 2, out_specs=[VMEM] * 2, vmem=56 * 2**20,
    )(flags, source_block, new_queries[:, 0], decode_queries)
    queries = exchange(query)

    width = decode_keys.shape[1]
    live = decode_lengths - tp * width
    part = decode_cache(
        live,
        dec_queries,
        decode_keys.reshape(4, width * 4, HD),
        decode_values.reshape(4, width * 4, HD),
    )

    queries, part = lax.optimization_barrier((queries, part))
    blocks = [(ctx & 18) + 4 * (k >> 1) + (k & 1) for k in range(QS)]
    blocks += [ctx ^ bits for bits in (0, 16, 3, 19)]
    meta = jnp.stack(blocks + [grp]).astype(i32)
    later, *sent = lax.optimization_barrier((pair, *sent))
    everyone = [pair, *sent, swap(later, 19)]
    acc0, acc1, sum0, sum1 = prefill_early(queries, everyone[:EARLY])
    first = prefill_late(0, meta, queries, everyone, acc0, sum0)
    meta, first = lax.optimization_barrier((meta, first))
    first_back = exchange(first)
    second = prefill_late(1, meta, queries, everyone, acc1, sum1)
    second_back = exchange(second)

    hand_back, second = lax.optimization_barrier((first_back, second))
    part = call(
        merge_hand_kernel, "merge_hand", struct((HD + 16, HD), i16), 3,
        in_specs=[SMEM] + [VMEM] * 2, out_specs=VMEM,
    )(flags, part, hand_back)
    parts = [part] + [lax.ppermute(part, "tp", [(i, i ^ k) for i in range(4)]) for k in (1, 2, 3)]
    out = call(
        combine_kernel, "combine", struct((TOK, 8 * HD), bf16), 2,
        cost=(2_000_000_000, 1_300_000, 10_000),
    )(first_back, second_back)
    decode_out = call(
        finish_kernel, "finish", struct((4, 4, 8 * HD), bf16), 5,
        scratch=[pltpu.VMEM((4, HD + 16, HD), i16), pltpu.VMEM((HD, HD), f32)],
        in_specs=[SMEM] + [VMEM] * 4, out_specs=VMEM,
    )(flags, *parts)
    return (out[:, None, :], decode_out)


def solution(mesh):
    in_specs = (
        P("ctx", ("tp", "grp"), None),
        P("ctx", ("tp", "grp"), None),
        P("ctx", ("tp", "grp"), None),
        P("ctx", ("tp", "grp"), None),
        P("ctx", ("tp", "grp"), None),
        P("ctx", "grp", None),
        P("ctx", "tp", "grp", None),
        P("ctx", "tp", "grp", None),
        P("ctx"),
        P("ctx"),
    )
    out_specs = (P("ctx", ("tp", "grp"), None), P("ctx", "grp", None))
    return jax.shard_map(local, mesh=mesh, in_specs=in_specs, out_specs=out_specs, check_vma=False)
```

```python
import functools
import math

import jax
import jax.numpy as jnp
from jax import lax
from jax.experimental import pallas as pl
from jax.experimental.pallas import tpu as pltpu
from jax.sharding import PartitionSpec as P

f32 = jnp.float32
bf16 = jnp.bfloat16
i16 = jnp.int16
i32 = jnp.int32

HD = 128
GROUPS = 8
TOK = 64
CACHE = 1024
QS = 8
KS = 4
NEWK = KS * TOK
PIECE = 512
TILE = 4 * TOK
SCALE2 = HD**-0.5 * math.log2(math.e)
NEG = -1e30
NOTHING = -1000.0
CODE = 32767.0
FIRST = 176
SECOND = 144
EARLY = 3
VMEM_LIMIT = 20 * 2**20
VMEM = pl.BlockSpec(memory_space=pltpu.VMEM)
SMEM = pl.BlockSpec(memory_space=pltpu.SMEM)


def contract_last(a, b):
    return lax.dot_general(a, b, (((1,), (1,)), ((), ())), preferred_element_type=f32)


def matmul(a, b):
    return jnp.dot(a, b, preferred_element_type=f32)


def split(p):
    high = p.astype(bf16)
    return high, (p - high.astype(f32)).astype(bf16)


def two_words(x):
    big = jnp.round(x * 32.0)
    return big, jnp.round((x * 32.0 - big) * 32768.0)


def one_number(big, small):
    return (big + small * (1.0 / 32768.0)) * (1.0 / 32.0)


def call(
    kernel, name, outs, count, scratch=(), cost=(1_000_000, 500_000, 1000), vmem=VMEM_LIMIT, **kwargs
):
    return pl.pallas_call(
        kernel,
        name=name,
        out_shape=outs,
        scratch_shapes=scratch,
        compiler_params=pltpu.CompilerParams(vmem_limit_bytes=vmem),
        cost_estimate=pl.CostEstimate(
            flops=cost[0], bytes_accessed=cost[1], transcendentals=cost[2]
        ),
        **kwargs,
    )


def keys_of(pair):
    return pair[0:CACHE, :]


def values_of(pair):
    return pair[CACHE : 2 * CACHE, :].T


def new_of(pairs, which):
    start = 2 * CACHE + which * TOK
    return jnp.concatenate([ref[start : start + TOK, :] for ref in pairs], 0)


def pack_query_kernel(source, new_queries, dec_queries, out, rows):
    tp, grp = lax.axis_index("tp"), lax.axis_index("grp")
    upper = (tp & 1) > 0
    mine, blocks = [], []
    for r in range(4):
        wide = dec_queries[r].astype(f32)
        heads = [
            jnp.concatenate([wide[j : j + 1, g * HD : (g + 1) * HD] for g in range(GROUPS)], 0)
            for j in range(4)
        ]
        rows[r] = jnp.concatenate(heads, 0).astype(bf16)
        mine += [jnp.where(upper, heads[2 + j], heads[j]) for j in range(2)]
        block = jnp.where(grp == (tp >> 1), source[r], -1).astype(f32)
        blocks.append(jnp.full((16, HD), block, f32).astype(bf16))
    mine = jnp.concatenate(mine, 0).astype(bf16)
    blocks = jnp.concatenate(blocks, 0)
    for s in range(QS):
        out[s, :, 0 : 8 * HD] = new_queries[...]
        out[s, :, 8 * HD : 9 * HD] = mine
        out[s, :, 9 * HD :] = blocks


def tile_queries(queries, b, half):
    start = half * (4 * HD)
    return jnp.concatenate(
        [queries[b, :, start + g * HD : start + (g + 1) * HD] for g in range(4)], 0
    )


def accumulate(tiles, states, blocks):
    work = [(i, t) for i in range(len(blocks)) for t in range(len(tiles))]
    states = list(states)
    following = contract_last(blocks[0][0](), tiles[0])
    for w, (i, t) in enumerate(work):
        scores = following
        if w + 1 < len(work):
            following = contract_last(blocks[work[w + 1][0]][0](), tiles[work[w + 1][1]])
        weights = jnp.exp2(scores * SCALE2)
        if blocks[i][2] is not None:
            weights = jnp.where(blocks[i][2][t], weights, 0.0)
        total, acc = states[t]
        total = total + jnp.sum(weights.reshape(-1, 8, TILE), 0)
        high, low = split(weights)
        values = blocks[i][1]()
        states[t] = (total, acc + matmul(values, high) + matmul(values, low))
    return states


def hand_off(meta, queries, pairs, out):
    rows = QS * 32
    lane = lax.broadcasted_iota(i32, (rows, HD), 1)
    pieces = [(s, r * 16) for s in range(QS) for r in range(4)]
    all_q = [queries[s, :, 8 * HD : 9 * HD].astype(f32) for s in range(QS)]
    all_source = [queries[s, :, 9 * HD :].astype(f32) for s in range(QS)]
    source = jnp.concatenate([all_source[s][a : a + 8] for s, a in pieces], 0)
    keep = jnp.concatenate(
        [
            source == jnp.where(lane < TOK, meta[QS + 2 * j], meta[QS + 2 * j + 1]).astype(f32)
            for j in range(2)
        ],
        1,
    )
    own = meta[QS + KS]
    results = []
    for head in range(2):
        hand_q = jnp.concatenate(
            [all_q[s][a + 8 * head : a + 8 * head + 8] for s, a in pieces], 0
        ).astype(bf16)
        keys = jnp.where(own == head, new_of(pairs, 0), new_of(pairs, 2))
        values = jnp.where(own == head, new_of(pairs, 1), new_of(pairs, 3))
        scores = jnp.where(keep, contract_last(hand_q, keys) * SCALE2, NEG)
        top = jnp.max(scores, 1, keepdims=True)
        weights = jnp.where(keep, jnp.exp2(scores - top), 0.0)
        total = jnp.sum(weights, 1, keepdims=True)
        both = matmul(jnp.concatenate(split(weights), 0), values)
        some = total > 0.0
        safe = jnp.where(some, total, 1.0)
        hand = (both[:rows] + both[rows:]) / safe
        lse = jnp.where(some, jnp.log2(safe) + top, NOTHING)
        most = jnp.maximum(jnp.max(jnp.abs(hand), 1, keepdims=True), 1e-30)
        hand = jnp.round(hand * (CODE / most))
        wide = [jnp.broadcast_to(x, (rows, HD)) for x in (lse, jnp.log2(most))]
        results.append((hand, [[x[:HD].T[0:1], x[HD:].T[0:1]] for x in wide]))
    sums = []
    for s in range(QS):
        slabs = [results[head][0][s * 32 : s * 32 + 32] for head in range(2)]
        out[s, HD + 16 : FIRST, :] = jnp.concatenate(slabs, 1).astype(i32).astype(i16)
        words = []
        for kind in range(2):
            place = s * 32 % HD
            pieces = [results[head][1][kind][s // 4][:, place : place + 32] for head in range(2)]
            row = jnp.concatenate(pieces + [jnp.zeros((1, TILE - 64), f32)], 1)
            words += [*two_words(row)]
        sums.append(words)
    return sums


def prefill_early_kernel(queries, *refs):
    pairs, (acc0, acc1, sum0, sum1, values_t) = refs[:EARLY], refs[EARLY:]
    for j, pair in enumerate(pairs):
        values_t[j] = values_of(pair)
    blocks = [
        (lambda j=j, n=n: pairs[j][n : n + PIECE, :], lambda j=j, n=n: values_t[j, :, n : n + PIECE], None)
        for j in range(EARLY)
        for n in range(0, CACHE, PIECE)
    ]

    def step(b, carry):
        tiles = [tile_queries(queries, b, half) for half in range(2)]
        zero = (jnp.zeros((8, TILE), f32), jnp.zeros((HD, TILE), f32))
        states = accumulate(tiles, [zero, zero], blocks)
        (sum0[b], acc0[b]), (sum1[b], acc1[b]) = states
        return carry

    lax.fori_loop(0, QS, step, 0)


def prefill_early(queries, pairs):
    outs = [jax.ShapeDtypeStruct((QS, HD, TILE), f32)] * 2
    outs += [jax.ShapeDtypeStruct((QS, 8, TILE), f32)] * 2
    return call(
        prefill_early_kernel, "prefill_early", outs, 1 + EARLY,
        scratch=[pltpu.VMEM((EARLY, HD, CACHE), bf16)],
        cost=(6 * 4096 * 1024 * EARLY * 128, 4_000_000, 4096 * 1024 * EARLY),
    )(queries, *pairs)


def prefill_late_kernel(half, meta, queries, *refs):
    pairs = refs[:KS]
    acc_in, sum_in, out, lse_all, most_all, values_t = refs[KS:]
    new_keys = new_of(pairs, 0)
    new_values_t = new_of(pairs, 1).T
    for j in range(EARLY, KS):
        values_t[j - EARLY] = values_of(pairs[j])
    cached = [
        (functools.partial(keys_of, pairs[j]), lambda j=j: values_t[j - EARLY], None)
        for j in range(EARLY, KS)
    ]

    def allowed(b):
        offset = lax.broadcasted_iota(i32, (TOK, TILE), 0)
        token = lax.broadcasted_iota(i32, (TOK, TILE), 1) & (TOK - 1)
        limit = token + meta[b] * TOK
        return jnp.concatenate([offset + meta[QS + j] * TOK <= limit for j in range(KS)], 0)

    def put(b, acc, total, top):
        most = jnp.maximum(jnp.max(jnp.abs(acc), 0, keepdims=True), 1e-30)
        out[b, 0:HD, :] = jnp.round(acc * (CODE / most)).astype(i32).astype(i16)
        size = jnp.log2(total)
        lse_all[b] = size + top
        most_all[b] = jnp.log2(most) - size

    def step(n, carry):
        places = [4 * n + k for k in range(4)]
        tiles = [tile_queries(queries, b, half) for b in places]
        new = (lambda: new_keys, lambda: new_values_t, [allowed(b) for b in places])
        states = [(sum_in[b], acc_in[b]) for b in places]
        for b, (total, acc) in zip(places, accumulate(tiles, states, cached + [new])):
            total = jnp.sum(total, 0, keepdims=True)
            put(b, acc, total, 0.0)
        return carry

    lax.fori_loop(0, QS // 4, step, 0)

    lse = lse_all[:, 0, :]
    outside = jnp.where((lse > -60.0) & (lse < 100.0), 0, 1)

    @pl.when(jnp.max(outside) > 0)
    def again():
        blocks = [
            (functools.partial(keys_of, pair), functools.partial(values_of, pair)) for pair in pairs
        ]
        blocks.append((lambda: new_keys, lambda: new_values_t))

        def one(b, carry):
            mask = allowed(b)
            tile = tile_queries(queries, b, half)
            top = jnp.full((1, TILE), NEG, f32)
            total = jnp.zeros((1, TILE), f32)
            acc = jnp.zeros((HD, TILE), f32)
            for i, block in enumerate(blocks):
                scores = contract_last(block[0](), tile) * SCALE2
                if i == KS:
                    scores = jnp.where(mask, scores, NEG)
                new_top = jnp.maximum(top, jnp.max(scores, 0, keepdims=True))
                weights = jnp.exp2(scores - new_top)
                factor = jnp.exp2(top - new_top)
                total = total * factor + jnp.sum(weights, 0, keepdims=True)
                first, second = split(weights)
                values = block[1]()
                acc = acc * factor + matmul(values, first) + matmul(values, second)
                top = new_top
            put(b, acc, total, top)
            return carry

        lax.fori_loop(0, QS, one, 0)

    if half == 0:
        hand_sums = hand_off(meta, queries, pairs, out)
    for s in range(QS):
        words = [*two_words(lse_all[s]), *two_words(most_all[s])]
        words += hand_sums[s] if half == 0 else []
        words += [jnp.zeros((16 - len(words), TILE), f32)]
        out[s, HD : HD + 16, :] = jnp.concatenate(words, 0).astype(i32).astype(i16)


def prefill_late(half, meta, queries, pairs, acc, total):
    return call(
        functools.partial(prefill_late_kernel, half),
        "prefill_second" if half else "prefill_first",
        jax.ShapeDtypeStruct((QS, SECOND if half else FIRST, TILE), i16), 8,
        scratch=[
            pltpu.VMEM((QS, 1, TILE), f32),
            pltpu.VMEM((QS, 1, TILE), f32),
            pltpu.VMEM((KS - EARLY, HD, CACHE), bf16),
        ],
        in_specs=[SMEM] + [VMEM] * 7,
        out_specs=VMEM,
        cost=(6 * 2048 * 1280 * 128, 4_000_000, 2048 * 1280),
    )(meta, queries, *pairs, acc, total)


def merge(outs, lses):
    top = functools.reduce(jnp.maximum, lses)
    factors = [jnp.exp2(x - top) for x in lses]
    total = sum(factors)
    return sum(o * w for o, w in zip(outs, factors)) / total, jnp.log2(total) + top


def combine_kernel(first, second, out):
    for half, parts in enumerate((first, second)):
        tails = [parts[s, HD : HD + 16, :].astype(i32).astype(f32) for s in range(QS)]
        lse = [one_number(tail[0:1], tail[1:2]) for tail in tails]
        most = [one_number(tail[2:3], tail[3:4]) for tail in tails]
        top = functools.reduce(jnp.maximum, lse)
        total = sum(jnp.exp2(x - top) for x in lse) * CODE
        acc = jnp.zeros((HD, TILE), f32)
        for s in range(QS):
            factor = jnp.exp2(lse[s] + most[s] - top) / total
            acc = acc + parts[s, 0:HD, :].astype(i32).astype(f32) * factor
        rows = acc.T
        for g in range(4):
            lanes = slice((half * 4 + g) * HD, (half * 4 + g + 1) * HD)
            out[:, lanes] = rows[g * TOK : (g + 1) * TOK].astype(bf16)


def as_row(wide):
    return wide.T[0:8]


def as_columns(row):
    return jnp.broadcast_to(row[0:1], (HD, HD)).T


def decode_kernel(meta, q_ref, k_ref, v_ref, out_ref, lse_ref):
    row = pl.program_id(0)
    scores = contract_last(q_ref[0], k_ref[0]) * SCALE2
    column = lax.broadcasted_iota(i32, scores.shape, 1)
    head = lax.broadcasted_iota(i32, scores.shape, 0) >> 3
    keep = ((column & 3) == head) & ((column >> 2) < meta[row])
    scores = jnp.where(keep, scores, NEG)
    top = jnp.max(scores, 1, keepdims=True)
    weights = jnp.where(keep, jnp.exp2(scores - top), 0.0)
    total = jnp.sum(weights, 1, keepdims=True)
    both = matmul(jnp.concatenate(split(weights), 0), v_ref[0])
    some = total > 0.0
    safe = jnp.where(some, total, 1.0)
    place = pl.ds(pl.multiple_of(row * 32, 32), 32)
    out_ref[place, :] = (both[0:32] + both[32:64]) / safe
    lse_ref[place, :] = jnp.broadcast_to(jnp.where(some, jnp.log2(safe) + top, NOTHING), (32, HD))

    @pl.when(row == 3)
    def last():
        out_ref[HD:, :] = as_row(lse_ref[...])


def decode_cache(live, queries, keys, values):
    rows, width, unused = keys.shape
    return call(
        decode_kernel, "decode_cache", jax.ShapeDtypeStruct((HD + 8, HD), f32), 4,
        scratch=[pltpu.VMEM((HD, HD), f32)],
        cost=(2_000_000_000, 4_400_000, 262_144),
        grid=(rows,),
        in_specs=[
            SMEM,
            pl.BlockSpec((1, 32, HD), lambda r: (r, 0, 0)),
            pl.BlockSpec((1, width, HD), lambda r: (r, 0, 0)),
            pl.BlockSpec((1, width, HD), lambda r: (r, 0, 0)),
        ],
        out_specs=pl.BlockSpec((HD + 8, HD), lambda r: (0, 0)),
    )(live, queries, keys, values)


def merge_hand_kernel(meta, part, back, out):
    tails = [back[s, HD : HD + 16, :].astype(i32).astype(f32)[4:8, 0:HD] for s in range(QS)]
    columns = jnp.concatenate(tails + [jnp.zeros((HD - 4 * QS, HD), f32)], 0).T
    slabs = [back[s, HD + 16 : FIRST, :].astype(i32).astype(f32) for s in range(QS)]
    heads = []
    for head in range(2):
        outs, sums = [], []
        for s in range(QS):
            four = [
                columns[head * 32 : head * 32 + 32, 4 * s + k : 4 * s + k + 1] for k in range(4)
            ]
            sums.append(one_number(four[0], four[1]))
            scale = jnp.exp2(one_number(four[2], four[3])) / CODE
            outs.append(slabs[s][:, head * HD : (head + 1) * HD] * scale)
        result, lse = merge(outs, sums)
        heads.append((result, jnp.broadcast_to(lse, (32, HD))))
    upper = meta[0] > 0
    blocks, lses = [], []
    for r in range(4):
        for j in range(4):
            fits = upper if j >= 2 else jnp.logical_not(upper)
            result, lse = (x[r * 8 : r * 8 + 8] for x in heads[j % 2])
            blocks.append(jnp.where(fits, result, 0.0))
            lses.append(jnp.where(fits, lse, NOTHING))
    result, lse = merge(
        [part[0:HD], jnp.concatenate(blocks, 0)],
        [as_columns(part[HD:]), jnp.concatenate(lses, 0)],
    )
    out[0:HD] = result
    out[HD:] = as_row(lse)


def finish_kernel(meta, *refs):
    parts, (out, placed, rows) = refs[:4], refs[4:]
    for k in range(4):
        placed[meta[2] ^ k] = parts[k][...]
    outs = [placed[t, 0:HD] for t in range(4)]
    rows[...] = merge(outs, [as_columns(placed[t, HD:]) for t in range(4)])[0]
    for r in range(4):
        for g in range(GROUPS):
            lanes = slice(g * HD, (g + 1) * HD)
            out[r, :, lanes] = rows[pl.ds(r * 32 + g, 4, stride=8), :].astype(bf16)


def local(
    new_queries,
    new_keys,
    new_values,
    cached_keys,
    cached_values,
    decode_queries,
    decode_keys,
    decode_values,
    decode_lengths,
    source_block,
):
    ctx = lax.axis_index("ctx")
    tp = lax.axis_index("tp")
    grp = lax.axis_index("grp")
    count = lax.axis_size("ctx")
    struct = jax.ShapeDtypeStruct

    def exchange(x):
        groups = [
            [z + 4 * (k >> 1) + y + (k & 1) for k in range(QS)] for z in (0, 16) for y in (0, 2)
        ]
        return lax.all_to_all(x, "ctx", 0, 0, axis_index_groups=groups, tiled=True)

    def other_core(x):
        return lax.ppermute(x, "grp", [(0, 1), (1, 0)])

    def swap(x, bits):
        return lax.ppermute(x, "ctx", [(i, i ^ bits) for i in range(count)])

    holds = (grp == (tp >> 1)).astype(i32)
    flags = jnp.stack([tp & 1, holds, tp]).astype(i32)
    query, dec_queries = call(
        pack_query_kernel, "pack_query",
        [struct((QS, TOK, 10 * HD), bf16), struct((4, 32, HD), bf16)], 4,
        in_specs=[SMEM] + [VMEM] * 2, out_specs=[VMEM] * 2, vmem=56 * 2**20,
    )(source_block, new_queries[:, 0], decode_queries)
    new_keys, new_values, query = lax.optimization_barrier((new_keys, new_values, query))
    queries = exchange(query)

    own_new = (new_keys[:, 0], new_values[:, 0])
    pair = jnp.concatenate(
        [cached_keys[:, 0], cached_values[:, 0], *own_new, *[other_core(x) for x in own_new]], 0
    )
    sent = [swap(pair, 16), swap(pair, 3)]

    width = decode_keys.shape[1]
    live = decode_lengths - tp * width
    part = decode_cache(
        live,
        dec_queries,
        decode_keys.reshape(4, width * 4, HD),
        decode_values.reshape(4, width * 4, HD),
    )

    later, part = lax.optimization_barrier((pair, part))
    everyone = [pair, *sent, swap(later, 19)]
    queries, part = lax.optimization_barrier((queries, part))
    blocks = [(ctx & 18) + 4 * (k >> 1) + (k & 1) for k in range(QS)]
    blocks += [ctx ^ bits for bits in (0, 16, 3, 19)]
    meta = jnp.stack(blocks + [grp]).astype(i32)
    acc0, acc1, sum0, sum1 = prefill_early(queries, everyone[:EARLY])
    first = prefill_late(0, meta, queries, everyone, acc0, sum0)
    meta, first = lax.optimization_barrier((meta, first))
    first_back = exchange(first)
    second = prefill_late(1, meta, queries, everyone, acc1, sum1)
    second_back = exchange(second)

    hand_back, second = lax.optimization_barrier((first_back, second))
    part = call(
        merge_hand_kernel, "merge_hand", struct((HD + 8, HD), f32), 3,
        in_specs=[SMEM] + [VMEM] * 2, out_specs=VMEM,
    )(flags, part, hand_back)
    parts = [part] + [lax.ppermute(part, "tp", [(i, i ^ k) for i in range(4)]) for k in (1, 2, 3)]
    out = call(
        combine_kernel, "combine", struct((TOK, 8 * HD), bf16), 2,
        cost=(2_000_000_000, 1_300_000, 10_000),
    )(first_back, second_back)
    decode_out = call(
        finish_kernel, "finish", struct((4, 4, 8 * HD), bf16), 5,
        scratch=[pltpu.VMEM((4, HD + 8, HD), f32), pltpu.VMEM((HD, HD), f32)],
        in_specs=[SMEM] + [VMEM] * 4, out_specs=VMEM,
    )(flags, *parts)
    return (out[:, None, :], decode_out)


def solution(mesh):
    in_specs = (
        P("ctx", ("tp", "grp"), None),
        P("ctx", ("tp", "grp"), None),
        P("ctx", ("tp", "grp"), None),
        P("ctx", ("tp", "grp"), None),
        P("ctx", ("tp", "grp"), None),
        P("ctx", "grp", None),
        P("ctx", "tp", "grp", None),
        P("ctx", "tp", "grp", None),
        P("ctx"),
        P("ctx"),
    )
    out_specs = (P("ctx", ("tp", "grp"), None), P("ctx", "grp", None))
    return jax.shard_map(local, mesh=mesh, in_specs=in_specs, out_specs=out_specs, check_vma=False)
```

```python
import functools
import math

import jax
import jax.numpy as jnp
from jax import lax
from jax.experimental import pallas as pl
from jax.experimental.pallas import tpu as pltpu
from jax.sharding import PartitionSpec as P

f32 = jnp.float32
bf16 = jnp.bfloat16
i16 = jnp.int16
i32 = jnp.int32

HD = 128
GROUPS = 8
TOK = 64
CACHE = 1024
QS = 8
KS = 4
NEWK = KS * TOK
PIECE = 512
TILE = 4 * TOK
SCALE2 = HD**-0.5 * math.log2(math.e)
NEG = -1e30
NOTHING = -1000.0
CODE = 32767.0
FIRST = 176
SECOND = 144
EARLY = 3
VMEM_LIMIT = 20 * 2**20
VMEM = pl.BlockSpec(memory_space=pltpu.VMEM)
SMEM = pl.BlockSpec(memory_space=pltpu.SMEM)


def contract_last(a, b):
    return lax.dot_general(a, b, (((1,), (1,)), ((), ())), preferred_element_type=f32)


def matmul(a, b):
    return jnp.dot(a, b, preferred_element_type=f32)


def split(p):
    high = p.astype(bf16)
    return high, (p - high.astype(f32)).astype(bf16)


def two_words(x):
    big = jnp.round(x * 32.0)
    return big, jnp.round((x * 32.0 - big) * 32768.0)


def one_number(big, small):
    return (big + small * (1.0 / 32768.0)) * (1.0 / 32.0)


def call(
    kernel, name, outs, count, scratch=(), cost=(1_000_000, 500_000, 1000), vmem=VMEM_LIMIT, **kwargs
):
    return pl.pallas_call(
        kernel,
        name=name,
        out_shape=outs,
        scratch_shapes=scratch,
        compiler_params=pltpu.CompilerParams(vmem_limit_bytes=vmem),
        cost_estimate=pl.CostEstimate(
            flops=cost[0], bytes_accessed=cost[1], transcendentals=cost[2]
        ),
        **kwargs,
    )


def keys_of(pair):
    return pair[0:CACHE, :]


def values_of(pair):
    return pair[CACHE : 2 * CACHE, :].T


def new_of(pairs, which):
    start = 2 * CACHE + which * TOK
    return jnp.concatenate([ref[start : start + TOK, :] for ref in pairs], 0)


def pack_query_kernel(source, new_queries, dec_queries, out, rows):
    tp, grp = lax.axis_index("tp"), lax.axis_index("grp")
    upper = (tp & 1) > 0
    mine, blocks = [], []
    for r in range(4):
        wide = dec_queries[r].astype(f32)
        heads = [
            jnp.concatenate([wide[j : j + 1, g * HD : (g + 1) * HD] for g in range(GROUPS)], 0)
            for j in range(4)
        ]
        rows[r] = jnp.concatenate(heads, 0).astype(bf16)
        mine += [jnp.where(upper, heads[2 + j], heads[j]) for j in range(2)]
        block = jnp.where(grp == (tp >> 1), source[r], -1).astype(f32)
        blocks.append(jnp.full((16, HD), block, f32).astype(bf16))
    mine = jnp.concatenate(mine, 0).astype(bf16)
    blocks = jnp.concatenate(blocks, 0)
    for s in range(QS):
        out[s, :, 0 : 8 * HD] = new_queries[...]
        out[s, :, 8 * HD : 9 * HD] = mine
        out[s, :, 9 * HD :] = blocks


def tile_queries(queries, b, half):
    start = half * (4 * HD)
    return jnp.concatenate(
        [queries[b, :, start + g * HD : start + (g + 1) * HD] for g in range(4)], 0
    )


def accumulate(tiles, states, blocks):
    work = [(i, t) for i in range(len(blocks)) for t in range(len(tiles))]
    states = list(states)
    following = contract_last(blocks[0][0](), tiles[0])
    for w, (i, t) in enumerate(work):
        scores = following
        if w + 1 < len(work):
            following = contract_last(blocks[work[w + 1][0]][0](), tiles[work[w + 1][1]])
        weights = jnp.exp2(scores * SCALE2)
        if blocks[i][2] is not None:
            weights = jnp.where(blocks[i][2][t], weights, 0.0)
        total, acc = states[t]
        total = total + jnp.sum(weights.reshape(-1, 8, TILE), 0)
        high, low = split(weights)
        values = blocks[i][1]()
        states[t] = (total, acc + matmul(values, high) + matmul(values, low))
    return states


def hand_off(meta, queries, pairs, out):
    rows = QS * 32
    lane = lax.broadcasted_iota(i32, (rows, HD), 1)
    pieces = [(s, r * 16) for s in range(QS) for r in range(4)]
    all_q = [queries[s, :, 8 * HD : 9 * HD].astype(f32) for s in range(QS)]
    all_source = [queries[s, :, 9 * HD :].astype(f32) for s in range(QS)]
    source = jnp.concatenate([all_source[s][a : a + 8] for s, a in pieces], 0)
    keep = jnp.concatenate(
        [
            source == jnp.where(lane < TOK, meta[QS + 2 * j], meta[QS + 2 * j + 1]).astype(f32)
            for j in range(2)
        ],
        1,
    )
    own = meta[QS + KS]
    results = []
    for head in range(2):
        hand_q = jnp.concatenate(
            [all_q[s][a + 8 * head : a + 8 * head + 8] for s, a in pieces], 0
        ).astype(bf16)
        keys = jnp.where(own == head, new_of(pairs, 0), new_of(pairs, 2))
        values = jnp.where(own == head, new_of(pairs, 1), new_of(pairs, 3))
        scores = jnp.where(keep, contract_last(hand_q, keys) * SCALE2, NEG)
        top = jnp.max(scores, 1, keepdims=True)
        weights = jnp.where(keep, jnp.exp2(scores - top), 0.0)
        total = jnp.sum(weights, 1, keepdims=True)
        both = matmul(jnp.concatenate(split(weights), 0), values)
        some = total > 0.0
        safe = jnp.where(some, total, 1.0)
        hand = (both[:rows] + both[rows:]) / safe
        lse = jnp.where(some, jnp.log2(safe) + top, NOTHING)
        most = jnp.maximum(jnp.max(jnp.abs(hand), 1, keepdims=True), 1e-30)
        hand = jnp.round(hand * (CODE / most))
        wide = [jnp.broadcast_to(x, (rows, HD)) for x in (lse, jnp.log2(most))]
        results.append((hand, [[x[:HD].T[0:1], x[HD:].T[0:1]] for x in wide]))
    sums = []
    for s in range(QS):
        slabs = [results[head][0][s * 32 : s * 32 + 32] for head in range(2)]
        out[s, HD + 16 : FIRST, :] = jnp.concatenate(slabs, 1).astype(i32).astype(i16)
        words = []
        for kind in range(2):
            place = s * 32 % HD
            pieces = [results[head][1][kind][s // 4][:, place : place + 32] for head in range(2)]
            row = jnp.concatenate(pieces + [jnp.zeros((1, TILE - 64), f32)], 1)
            words += [*two_words(row)]
        sums.append(words)
    return sums


def prefill_early_kernel(queries, *refs):
    pairs, (acc0, acc1, sum0, sum1, values_t) = refs[:EARLY], refs[EARLY:]
    for j, pair in enumerate(pairs):
        values_t[j] = values_of(pair)
    blocks = [
        (lambda j=j, n=n: pairs[j][n : n + PIECE, :], lambda j=j, n=n: values_t[j, :, n : n + PIECE], None)
        for j in range(EARLY)
        for n in range(0, CACHE, PIECE)
    ]

    def step(b, carry):
        tiles = [tile_queries(queries, b, half) for half in range(2)]
        zero = (jnp.zeros((8, TILE), f32), jnp.zeros((HD, TILE), f32))
        states = accumulate(tiles, [zero, zero], blocks)
        (sum0[b], acc0[b]), (sum1[b], acc1[b]) = states
        return carry

    lax.fori_loop(0, QS, step, 0)


def prefill_early(queries, pairs):
    outs = [jax.ShapeDtypeStruct((QS, HD, TILE), f32)] * 2
    outs += [jax.ShapeDtypeStruct((QS, 8, TILE), f32)] * 2
    return call(
        prefill_early_kernel, "prefill_early", outs, 1 + EARLY,
        scratch=[pltpu.VMEM((EARLY, HD, CACHE), bf16)],
        cost=(6 * 4096 * 1024 * EARLY * 128, 4_000_000, 4096 * 1024 * EARLY),
    )(queries, *pairs)


def prefill_late_kernel(half, meta, queries, *refs):
    pairs = refs[:KS]
    acc_in, sum_in, out, lse_all, most_all, values_t = refs[KS:]
    new_keys = new_of(pairs, 0)
    new_values_t = new_of(pairs, 1).T
    for j in range(EARLY, KS):
        values_t[j - EARLY] = values_of(pairs[j])
    cached = [
        (
            lambda j=j, n=n: pairs[j][n : n + PIECE, :],
            lambda j=j, n=n: values_t[j - EARLY, :, n : n + PIECE],
            None,
        )
        for j in range(EARLY, KS)
        for n in range(0, CACHE, PIECE)
    ]

    def allowed(b):
        offset = lax.broadcasted_iota(i32, (TOK, TILE), 0)
        token = lax.broadcasted_iota(i32, (TOK, TILE), 1) & (TOK - 1)
        limit = token + meta[b] * TOK
        return jnp.concatenate([offset + meta[QS + j] * TOK <= limit for j in range(KS)], 0)

    def put(b, acc, total, top):
        most = jnp.maximum(jnp.max(jnp.abs(acc), 0, keepdims=True), 1e-30)
        out[b, 0:HD, :] = jnp.round(acc * (CODE / most)).astype(i32).astype(i16)
        size = jnp.log2(total)
        lse_all[b] = size + top
        most_all[b] = jnp.log2(most) - size

    def step(n, carry):
        places = [4 * n + k for k in range(4)]
        tiles = [tile_queries(queries, b, half) for b in places]
        new = (lambda: new_keys, lambda: new_values_t, [allowed(b) for b in places])
        states = [(sum_in[b], acc_in[b]) for b in places]
        for b, (total, acc) in zip(places, accumulate(tiles, states, cached + [new])):
            total = jnp.sum(total, 0, keepdims=True)
            put(b, acc, total, 0.0)
        return carry

    lax.fori_loop(0, QS // 4, step, 0)

    lse = lse_all[:, 0, :]
    outside = jnp.where((lse > -60.0) & (lse < 100.0), 0, 1)

    @pl.when(jnp.max(outside) > 0)
    def again():
        blocks = [
            (functools.partial(keys_of, pair), functools.partial(values_of, pair)) for pair in pairs
        ]
        blocks.append((lambda: new_keys, lambda: new_values_t))

        def one(b, carry):
            mask = allowed(b)
            tile = tile_queries(queries, b, half)
            top = jnp.full((1, TILE), NEG, f32)
            total = jnp.zeros((1, TILE), f32)
            acc = jnp.zeros((HD, TILE), f32)
            for i, block in enumerate(blocks):
                scores = contract_last(block[0](), tile) * SCALE2
                if i == KS:
                    scores = jnp.where(mask, scores, NEG)
                new_top = jnp.maximum(top, jnp.max(scores, 0, keepdims=True))
                weights = jnp.exp2(scores - new_top)
                factor = jnp.exp2(top - new_top)
                total = total * factor + jnp.sum(weights, 0, keepdims=True)
                first, second = split(weights)
                values = block[1]()
                acc = acc * factor + matmul(values, first) + matmul(values, second)
                top = new_top
            put(b, acc, total, top)
            return carry

        lax.fori_loop(0, QS, one, 0)

    if half == 0:
        hand_sums = hand_off(meta, queries, pairs, out)
    for s in range(QS):
        words = [*two_words(lse_all[s]), *two_words(most_all[s])]
        words += hand_sums[s] if half == 0 else []
        words += [jnp.zeros((16 - len(words), TILE), f32)]
        out[s, HD : HD + 16, :] = jnp.concatenate(words, 0).astype(i32).astype(i16)


def prefill_late(half, meta, queries, pairs, acc, total):
    return call(
        functools.partial(prefill_late_kernel, half),
        "prefill_second" if half else "prefill_first",
        jax.ShapeDtypeStruct((QS, SECOND if half else FIRST, TILE), i16), 8,
        scratch=[
            pltpu.VMEM((QS, 1, TILE), f32),
            pltpu.VMEM((QS, 1, TILE), f32),
            pltpu.VMEM((KS - EARLY, HD, CACHE), bf16),
        ],
        in_specs=[SMEM] + [VMEM] * 7,
        out_specs=VMEM,
        cost=(6 * 2048 * 1280 * 128, 4_000_000, 2048 * 1280),
    )(meta, queries, *pairs, acc, total)


def merge(outs, lses):
    top = functools.reduce(jnp.maximum, lses)
    factors = [jnp.exp2(x - top) for x in lses]
    total = sum(factors)
    return sum(o * w for o, w in zip(outs, factors)) / total, jnp.log2(total) + top


def combine_kernel(first, second, out):
    for half, parts in enumerate((first, second)):
        tails = [parts[s, HD : HD + 16, :].astype(i32).astype(f32) for s in range(QS)]
        lse = [one_number(tail[0:1], tail[1:2]) for tail in tails]
        most = [one_number(tail[2:3], tail[3:4]) for tail in tails]
        top = functools.reduce(jnp.maximum, lse)
        total = sum(jnp.exp2(x - top) for x in lse) * CODE
        acc = jnp.zeros((HD, TILE), f32)
        for s in range(QS):
            factor = jnp.exp2(lse[s] + most[s] - top) / total
            acc = acc + parts[s, 0:HD, :].astype(i32).astype(f32) * factor
        rows = acc.T
        for g in range(4):
            lanes = slice((half * 4 + g) * HD, (half * 4 + g + 1) * HD)
            out[:, lanes] = rows[g * TOK : (g + 1) * TOK].astype(bf16)


def as_row(wide):
    return wide.T[0:8]


def as_columns(row):
    return jnp.broadcast_to(row[0:1], (HD, HD)).T


def decode_kernel(meta, q_ref, k_ref, v_ref, out_ref, lse_ref):
    row = pl.program_id(0)
    scores = contract_last(q_ref[0], k_ref[0]) * SCALE2
    column = lax.broadcasted_iota(i32, scores.shape, 1)
    head = lax.broadcasted_iota(i32, scores.shape, 0) >> 3
    keep = ((column & 3) == head) & ((column >> 2) < meta[row])
    scores = jnp.where(keep, scores, NEG)
    top = jnp.max(scores, 1, keepdims=True)
    weights = jnp.where(keep, jnp.exp2(scores - top), 0.0)
    total = jnp.sum(weights, 1, keepdims=True)
    both = matmul(jnp.concatenate(split(weights), 0), v_ref[0])
    some = total > 0.0
    safe = jnp.where(some, total, 1.0)
    place = pl.ds(pl.multiple_of(row * 32, 32), 32)
    out_ref[place, :] = (both[0:32] + both[32:64]) / safe
    lse_ref[place, :] = jnp.broadcast_to(jnp.where(some, jnp.log2(safe) + top, NOTHING), (32, HD))

    @pl.when(row == 3)
    def last():
        out_ref[HD:, :] = as_row(lse_ref[...])


def decode_cache(live, queries, keys, values):
    rows, width, unused = keys.shape
    return call(
        decode_kernel, "decode_cache", jax.ShapeDtypeStruct((HD + 8, HD), f32), 4,
        scratch=[pltpu.VMEM((HD, HD), f32)],
        cost=(2_000_000_000, 4_400_000, 262_144),
        grid=(rows,),
        in_specs=[
            SMEM,
            pl.BlockSpec((1, 32, HD), lambda r: (r, 0, 0)),
            pl.BlockSpec((1, width, HD), lambda r: (r, 0, 0)),
            pl.BlockSpec((1, width, HD), lambda r: (r, 0, 0)),
        ],
        out_specs=pl.BlockSpec((HD + 8, HD), lambda r: (0, 0)),
    )(live, queries, keys, values)


def merge_hand_kernel(meta, part, back, out):
    tails = [back[s, HD : HD + 16, :].astype(i32).astype(f32)[4:8, 0:HD] for s in range(QS)]
    columns = jnp.concatenate(tails + [jnp.zeros((HD - 4 * QS, HD), f32)], 0).T
    slabs = [back[s, HD + 16 : FIRST, :].astype(i32).astype(f32) for s in range(QS)]
    heads = []
    for head in range(2):
        outs, sums = [], []
        for s in range(QS):
            four = [
                columns[head * 32 : head * 32 + 32, 4 * s + k : 4 * s + k + 1] for k in range(4)
            ]
            sums.append(one_number(four[0], four[1]))
            scale = jnp.exp2(one_number(four[2], four[3])) / CODE
            outs.append(slabs[s][:, head * HD : (head + 1) * HD] * scale)
        result, lse = merge(outs, sums)
        heads.append((result, jnp.broadcast_to(lse, (32, HD))))
    upper = meta[0] > 0
    blocks, lses = [], []
    for r in range(4):
        for j in range(4):
            fits = upper if j >= 2 else jnp.logical_not(upper)
            result, lse = (x[r * 8 : r * 8 + 8] for x in heads[j % 2])
            blocks.append(jnp.where(fits, result, 0.0))
            lses.append(jnp.where(fits, lse, NOTHING))
    result, lse = merge(
        [part[0:HD], jnp.concatenate(blocks, 0)],
        [as_columns(part[HD:]), jnp.concatenate(lses, 0)],
    )
    out[0:HD] = result
    out[HD:] = as_row(lse)


def finish_kernel(meta, *refs):
    parts, (out, placed, rows) = refs[:4], refs[4:]
    for k in range(4):
        placed[meta[2] ^ k] = parts[k][...]
    outs = [placed[t, 0:HD] for t in range(4)]
    rows[...] = merge(outs, [as_columns(placed[t, HD:]) for t in range(4)])[0]
    for r in range(4):
        for g in range(GROUPS):
            lanes = slice(g * HD, (g + 1) * HD)
            out[r, :, lanes] = rows[pl.ds(r * 32 + g, 4, stride=8), :].astype(bf16)


def local(
    new_queries,
    new_keys,
    new_values,
    cached_keys,
    cached_values,
    decode_queries,
    decode_keys,
    decode_values,
    decode_lengths,
    source_block,
):
    ctx = lax.axis_index("ctx")
    tp = lax.axis_index("tp")
    grp = lax.axis_index("grp")
    count = lax.axis_size("ctx")
    struct = jax.ShapeDtypeStruct

    def exchange(x):
        groups = [
            [z + 4 * (k >> 1) + y + (k & 1) for k in range(QS)] for z in (0, 16) for y in (0, 2)
        ]
        return lax.all_to_all(x, "ctx", 0, 0, axis_index_groups=groups, tiled=True)

    def other_core(x):
        return lax.ppermute(x, "grp", [(0, 1), (1, 0)])

    def swap(x, bits):
        return lax.ppermute(x, "ctx", [(i, i ^ bits) for i in range(count)])

    holds = (grp == (tp >> 1)).astype(i32)
    flags = jnp.stack([tp & 1, holds, tp]).astype(i32)
    query, dec_queries = call(
        pack_query_kernel, "pack_query",
        [struct((QS, TOK, 10 * HD), bf16), struct((4, 32, HD), bf16)], 4,
        in_specs=[SMEM] + [VMEM] * 2, out_specs=[VMEM] * 2, vmem=56 * 2**20,
    )(source_block, new_queries[:, 0], decode_queries)
    new_keys, new_values, query = lax.optimization_barrier((new_keys, new_values, query))
    queries = exchange(query)

    own_new = (new_keys[:, 0], new_values[:, 0])
    pair = jnp.concatenate(
        [cached_keys[:, 0], cached_values[:, 0], *own_new, *[other_core(x) for x in own_new]], 0
    )
    sent = [swap(pair, 16), swap(pair, 3)]

    width = decode_keys.shape[1]
    live = decode_lengths - tp * width
    part = decode_cache(
        live,
        dec_queries,
        decode_keys.reshape(4, width * 4, HD),
        decode_values.reshape(4, width * 4, HD),
    )

    later, part = lax.optimization_barrier((pair, part))
    everyone = [pair, *sent, swap(later, 19)]
    queries, part = lax.optimization_barrier((queries, part))
    blocks = [(ctx & 18) + 4 * (k >> 1) + (k & 1) for k in range(QS)]
    blocks += [ctx ^ bits for bits in (0, 16, 3, 19)]
    meta = jnp.stack(blocks + [grp]).astype(i32)
    acc0, acc1, sum0, sum1 = prefill_early(queries, everyone[:EARLY])
    first = prefill_late(0, meta, queries, everyone, acc0, sum0)
    meta, first = lax.optimization_barrier((meta, first))
    first_back = exchange(first)
    second = prefill_late(1, meta, queries, everyone, acc1, sum1)
    second_back = exchange(second)

    hand_back, second = lax.optimization_barrier((first_back, second))
    part = call(
        merge_hand_kernel, "merge_hand", struct((HD + 8, HD), f32), 3,
        in_specs=[SMEM] + [VMEM] * 2, out_specs=VMEM,
    )(flags, part, hand_back)
    parts = [part] + [lax.ppermute(part, "tp", [(i, i ^ k) for i in range(4)]) for k in (1, 2, 3)]
    out = call(
        combine_kernel, "combine", struct((TOK, 8 * HD), bf16), 2,
        cost=(2_000_000_000, 1_300_000, 10_000),
    )(first_back, second_back)
    decode_out = call(
        finish_kernel, "finish", struct((4, 4, 8 * HD), bf16), 5,
        scratch=[pltpu.VMEM((4, HD + 8, HD), f32), pltpu.VMEM((HD, HD), f32)],
        in_specs=[SMEM] + [VMEM] * 4, out_specs=VMEM,
    )(flags, *parts)
    return (out[:, None, :], decode_out)


def solution(mesh):
    in_specs = (
        P("ctx", ("tp", "grp"), None),
        P("ctx", ("tp", "grp"), None),
        P("ctx", ("tp", "grp"), None),
        P("ctx", ("tp", "grp"), None),
        P("ctx", ("tp", "grp"), None),
        P("ctx", "grp", None),
        P("ctx", "tp", "grp", None),
        P("ctx", "tp", "grp", None),
        P("ctx"),
        P("ctx"),
    )
    out_specs = (P("ctx", ("tp", "grp"), None), P("ctx", "grp", None))
    return jax.shard_map(local, mesh=mesh, in_specs=in_specs, out_specs=out_specs, check_vma=False)
```
